32 devices in a mesh: slab: 8 (over z, x), grp: 4 (over y, core).
Axes of the slice: x: 2, y: 2, z: 4, core: 2. Of those that a mesh axis runs over, the one named last changes fastest.
Arguments:
- a_blocks: bfloat16 [8192, 7, 4096], P(('slab', 'grp')), may hold values from -1.5 to 1.5
- a_cols: int32 [8192, 7], P(('slab', 'grp')), may hold values from 0 to 8191, as said below
- p_blocks: bfloat16 [8192, 4096], P(('slab', 'grp')), may hold values from -0.75 to 0.75
- p_cols: int32 [8192], P(('slab', 'grp')), may hold values from 0 to 1023, as said below
- coarse_owner: int32 [32, 32], replicated, may hold values from 0 to 31, each once within a row
Outputs:
- coarse_blocks: bfloat16 [1024, 7, 4096], P(('slab', 'grp'))
The draws below stay inside these ranges and needn't reach their ends.
Inputs may be any that keep to these rules, and one draw needn't show every extreme that they name: `a_cols`: fine block row f is the block at layer z = f // 128, y = (f // 8) mod 16, x = f mod 8; its row lists its own block and the six blocks at x +- 1 mod 8, y +- 1 mod 16, z +- 1 mod 64, each once, in any order. 8 distinct cut positions among the y values split y cyclically into 8 runs, the same in every layer and column; run = (number of cuts <= y) - 1 mod 8. The block at (z, y, x) has p_cols = (((z + 1) // 2) mod 32) * 32 + (x // 2) * 8 + run. `coarse_owner`: each row is a permutation.
All inputs are finite; a program needn't handle non-finite values.
Results may differ from the reference program's by a relative error of at most 0.0049.
Values may be sent and summed in bfloat16 or wider, within the bound.
A program may use at most 320 MiB of HBM per device.

```python
import jax
import jax.numpy as jnp
from jax import lax

BS = 64
KA = 7
KC = 7
PX = 8
PY = 16
RUNS = 8
AXY = 32
CPS = 4
NZA = 32
GZ = 64
FB = 256
NF = 8192
NC = 1024
N_SLAB = 8
N_GRP = 4


def draw_a_cols(key, part):
    key = jax.random.fold_in(key, 11)
    index = jnp.arange(NF, dtype=jnp.int32)
    xpos = index % PX
    ypos = index // PX % PY
    zpos = index // (PX * PY)

    def locate(zz, yy, xx):
        return (zz % GZ * PY + yy % PY) * PX + xx % PX
    beside_all = jnp.stack([locate(zpos, ypos, xpos), locate(zpos, ypos, xpos - 1), locate(zpos, ypos, xpos + 1), locate(zpos, ypos - 1, xpos), locate(zpos, ypos + 1, xpos), locate(zpos - 1, ypos, xpos), locate(zpos + 1, ypos, xpos)], axis=1)
    scores = jax.random.randint(key, (NF, KA), 0, 1 << 20) * KA + jnp.arange(KA, dtype=jnp.int32)[None, :]
    order = jnp.argsort(scores, axis=1, stable=True)
    return jnp.take_along_axis(beside_all, order, axis=1).astype(jnp.int32)


def draw_p_cols(key, part):
    key = jax.random.fold_in(key, 12)
    scores = jax.random.randint(key, (PY,), 0, 1 << 20) * PY + jnp.arange(PY, dtype=jnp.int32)
    picked = jnp.argsort(scores, stable=True)[:RUNS]
    cuts = jnp.sort(picked).astype(jnp.int32)
    index = jnp.arange(NF, dtype=jnp.int32)
    xpos = index % PX
    ypos = index // PX % PY
    zpos = index // (PX * PY)
    counted = jnp.sum((cuts[None, :] <= ypos[:, None]).astype(jnp.int32), axis=1)
    within = (counted - 1) % RUNS
    layer = (zpos + 1) // 2 % NZA
    return (layer * AXY + xpos // 2 * RUNS + within).astype(jnp.int32)


def block_scale(stream_key, shape, split, least, high):
    def one(axis_at, parts):
        heights = jax.random.uniform(jax.random.fold_in(jax.random.fold_in(stream_key, 6), axis_at), (parts,), jnp.float32, least / len(split), high / len(split))
        return jnp.repeat(jnp.exp(heights), shape[axis_at] // parts).reshape((-1,) + (1,) * (len(shape) - axis_at - 1))

    level = one(*split[0])
    for cut in split[1:]:
        level = level * one(*cut)
    return level


def normal_values(rng, shape, deviation, limit, shards=(), held_as=jnp.bfloat16):
    array = deviation * jax.random.normal(rng, shape, jnp.float32)
    if shards:
        array = array * block_scale(rng, shape, shards, -0.22, 0.18)
    return jnp.clip(array, -limit, limit).astype(held_as)


def setup_inputs(seed: int = 0) -> dict:
    key_list = jax.random.split(jax.random.key(seed), 6)
    a_blocks = normal_values(key_list[0], (NF, KA, BS * BS), 0.25, 1.5, ((0, 32),))
    a_cols = draw_a_cols(jax.random.fold_in(key_list[5], 71), 0)
    p_blocks = normal_values(key_list[2], (NF, BS * BS), BS ** -0.5, 0.75, ((0, 32),))
    p_cols = draw_p_cols(jax.random.fold_in(key_list[5], 71), 0)
    coarse_owner = jax.vmap(lambda own: jax.random.permutation(own, AXY))(jax.random.split(key_list[4], NZA)).reshape((NZA, AXY)).astype(jnp.int32)
    return dict(a_blocks=a_blocks, a_cols=a_cols, p_blocks=p_blocks, p_cols=p_cols, coarse_owner=coarse_owner)


def slot_of(q_from, a_from, q_to, a_to, layer_count):
    column = q_from // RUNS
    within = q_from % RUNS
    columns = PX // 2
    left_q = ((column - 1) % columns) * RUNS + within
    right_q = ((column + 1) % columns) * RUNS + within
    down_q = column * RUNS + (within - 1) % RUNS
    upper_q = column * RUNS + (within + 1) % RUNS
    result = jnp.where(q_to == left_q, 1, jnp.where(q_to == right_q, 2, jnp.where(q_to == down_q, 3, jnp.where(q_to == upper_q, 4, 0))))
    drift = (a_to - a_from) % layer_count
    return jnp.where(drift == 1, 6, jnp.where(drift == layer_count - 1, 5, result)).astype(jnp.int32)


def reference(a_blocks, a_cols, p_blocks, p_cols, coarse_owner):
    prolong = p_blocks.reshape(NF, BS, BS)

    def one_slab(accumulated, first_row):
        blocks = lax.dynamic_slice_in_dim(a_blocks, first_row, FB, 0).reshape(FB, KA, BS, BS).astype(jnp.float32)
        columns = lax.dynamic_slice_in_dim(a_cols, first_row, FB, 0)
        target = lax.dynamic_slice_in_dim(p_cols, first_row, FB, 0)
        own_prolong = lax.dynamic_slice_in_dim(prolong, first_row, FB, 0).astype(jnp.float32)
        fetched = prolong[columns].astype(jnp.float32)
        carried = jnp.einsum("fkab,fkbc->fkac", blocks, fetched).astype(jnp.bfloat16)
        carried = lax.optimization_barrier(carried).astype(jnp.float32)
        products = jnp.einsum("fba,fkbc->fkac", own_prolong, carried)
        dest_c = p_cols[columns]
        slot = slot_of(target[:, None] % AXY, target[:, None] // AXY, dest_c % AXY, dest_c // AXY, NZA)
        segment = (target[:, None] * KC + slot).reshape(-1)
        accumulated = accumulated.at[segment].add(products.reshape(FB * KA, BS * BS))
        return accumulated, None

    starts = jnp.arange(NZA, dtype=jnp.int32) * FB
    accumulated = jnp.zeros((NC * KC, BS * BS), jnp.float32)
    accumulated, _ = lax.scan(one_slab, accumulated, starts)
    owners = coarse_owner.reshape(-1)
    layer_index = jnp.arange(NC, dtype=jnp.int32) // AXY
    placed = (((owners // CPS) * N_GRP + layer_index % N_GRP) * N_SLAB + layer_index // N_GRP) * CPS + owners % CPS
    result = jnp.zeros((NC, KC, BS * BS), jnp.bfloat16)
    return result.at[placed].set(accumulated.reshape(NC, KC, BS * BS).astype(jnp.bfloat16))
```

```python
import functools

import jax
import jax.numpy as jnp
from jax import lax
from jax.experimental import pallas as pl
from jax.experimental.pallas import tpu as pltpu
from jax.sharding import PartitionSpec as P

KC = 7
PX = 8
PY = 16
RUNS = 8
AXY = 32
PLANE = PX * PY
BS = 64
HALF = BS // 2
WIDE = 2 * BS
RUN_AT = PLANE * KC
DOWN_AT = RUN_AT + PY
UP_AT = DOWN_AT + PY
PICK_AT = UP_AT + PY
F32 = jnp.float32
BF16 = jnp.bfloat16


def layer_kernel(
    out_slot, zero_slot, scal, a_ref, own_ref, zin_ref, zout_ref, out_ref,
    tmp, ptmp, vtmp, arel, prel, plhs, carried, acc,
):
    step = pl.program_id(0)
    rows = a_ref.shape[0]
    lane = lax.broadcasted_iota(jnp.int32, (HALF, WIDE), 1)
    low = lane < BS

    def swap(x):
        return pltpu.roll(x, BS, 1)

    for r in range(rows):
        for i in range(HALF):
            tmp[r, i * 8 : i * 8 + KC, :] = a_ref[r, :, i * WIDE : (i + 1) * WIDE].astype(F32)
    for r in range(rows):
        f = step * rows + r
        for j in range(KC):
            k = scal[f * KC + j]
            arel[j, f] = tmp[r, pl.ds(k, HALF, stride=8), :].astype(BF16)

    for t, ref in enumerate((own_ref, zin_ref, zout_ref)):
        for i in range(HALF):
            ptmp[t, i * rows : (i + 1) * rows, :] = ref[:, i * WIDE : (i + 1) * WIDE].astype(F32)
        for r in range(rows):
            f = step * rows + r
            val = ptmp[t, pl.ds(r, HALF, stride=rows), :]
            turned = swap(val)
            vtmp[t, r, pl.ds(0, HALF, stride=2), :] = jnp.where(low, val, turned)
            vtmp[t, r, pl.ds(1, HALF, stride=2), :] = jnp.where(low, turned, val)
            prel[t, f] = vtmp[t, r].astype(BF16)
            if t == 0:
                plhs[f // 2, r % 2, 0] = val.astype(BF16)
                plhs[f // 2, r % 2, 1] = turned.astype(BF16)

    @pl.when(step == pl.num_programs(0) - 1)
    def _():
        lane2 = lax.broadcasted_iota(jnp.int32, (BS, WIDE), 1)
        low2 = lane2 < BS

        def both(t, g):
            dup = prel[t, g].astype(F32)
            top = jnp.where(low2, dup, 0.0)
            bottom = jnp.where(low2, 0.0, dup)
            return jnp.concatenate([top, bottom], axis=0).astype(BF16)

        def carry_row(y, _):
            above = lax.rem(y + 1, PY)
            below = lax.rem(y + PY - 1, PY)
            for x in range(PX):
                g = y * PX + x
                takers = (
                    (0, g),
                    (1, y * PX + (x + 1) % PX),
                    (2, y * PX + (x - 1) % PX),
                    (3, above * PX + x),
                    (4, below * PX + x),
                )
                lhs = jnp.concatenate([arel[j, f] for j, f in takers], axis=0)
                got = jnp.dot(lhs, both(0, g), preferred_element_type=F32).astype(BF16)
                for n, (j, f) in enumerate(takers):
                    carried[j, f] = got[n * HALF : (n + 1) * HALF]
                for t in (1, 2):
                    carried[4 + t, g] = jnp.dot(
                        arel[4 + t, g], both(t, g), preferred_element_type=F32
                    ).astype(BF16)
            return 0

        lax.fori_loop(0, PY, carry_row, 0)

        acc[...] = jnp.zeros_like(acc)

        def pair(a, b):
            return jnp.concatenate(
                [jnp.where(low, a, swap(b)), jnp.where(low, swap(a), b)], axis=0
            ).astype(BF16)

        def sum_row(y, _):
            run = scal[RUN_AT + y]
            down_in = scal[DOWN_AT + y] != 0
            up_in = scal[UP_AT + y] != 0
            zero = jnp.zeros((HALF, WIDE), F32)
            for c in range(PX // 2):
                parts = ([], [], [])
                for e in range(2):
                    f = y * PX + 2 * c + e
                    own, left, right, down, up, zin, zout = (
                        carried[j, f].astype(F32) for j in range(KC)
                    )
                    inner, outer = (right, left) if e == 0 else (left, right)
                    kept = (own + inner) + zin
                    kept = kept + jnp.where(down_in, down, zero) + jnp.where(up_in, up, zero)
                    down = jnp.where(down_in, zero, down)
                    up = jnp.where(up_in, zero, up)
                    parts[0].append(pair(kept, zout))
                    parts[1].append(pair(down, up))
                    parts[2].append(pair(outer, zero) if e == 0 else pair(zero, outer))
                at = (y * PX) // 2 + c
                lhs = plhs[at].reshape(2 * BS, WIDE)[:, :BS]
                q = c * RUNS + run
                for b in range(3):
                    acc[q, b] += lax.dot_general(
                        lhs,
                        jnp.concatenate(parts[b], axis=0),
                        (((0,), (0,)), ((), ())),
                        preferred_element_type=F32,
                    )
            return 0

        lax.fori_loop(0, PY, sum_row, 0)

        slots = ((0, out_slot), (3, 4), (1, 2))

        def write_row(o, _):
            q = scal[PICK_AT + o]
            for b in range(3):
                even = acc[q, b, pl.ds(0, HALF, stride=2), :]
                odd = acc[q, b, pl.ds(1, HALF, stride=2), :]
                tmp[0, pl.ds(slots[b][0], HALF, stride=8), :] = jnp.where(low, even, swap(odd))
                tmp[0, pl.ds(slots[b][1], HALF, stride=8), :] = jnp.where(low, swap(even), odd)
            tmp[0, pl.ds(zero_slot, HALF, stride=8), :] = jnp.zeros((HALF, WIDE), F32)
            for i in range(HALF):
                out_ref[o, :, i * WIDE : (i + 1) * WIDE] = tmp[0, i * 8 : i * 8 + KC, :].astype(
                    out_ref.dtype
                )
            return 0

        lax.fori_loop(0, AXY, write_row, 0)


def layer_part(a_blocks, layer, scalars, own, zin, zout, out_slot, zero_slot, dtype):
    rows = 16
    steps = PLANE // rows
    flat = BS * BS
    plane_spec = pl.BlockSpec((rows, flat), lambda s, _: (s, 0))
    return pl.pallas_call(
        functools.partial(layer_kernel, out_slot, zero_slot),
        out_shape=jax.ShapeDtypeStruct((AXY, KC, flat), dtype),
        grid_spec=pltpu.PrefetchScalarGridSpec(
            num_scalar_prefetch=1,
            grid=(steps,),
            in_specs=[
                pl.BlockSpec((rows, KC, flat), lambda s, _: (layer * steps + s, 0, 0)),
                plane_spec,
                plane_spec,
                plane_spec,
            ],
            out_specs=pl.BlockSpec((AXY, KC, flat), lambda s, _: (0, 0, 0)),
            scratch_shapes=[
                pltpu.VMEM((rows, 8 * HALF, WIDE), F32),
                pltpu.VMEM((3, rows * HALF, WIDE), F32),
                pltpu.VMEM((3, rows, BS, WIDE), F32),
                pltpu.VMEM((KC, PLANE, HALF, WIDE), BF16),
                pltpu.VMEM((3, PLANE, BS, WIDE), BF16),
                pltpu.VMEM((PLANE // 2, 2, 2, HALF, WIDE), BF16),
                pltpu.VMEM((KC, PLANE, HALF, WIDE), BF16),
                pltpu.VMEM((AXY, 3, BS, WIDE), F32),
            ],
        ),
        compiler_params=pltpu.CompilerParams(vmem_limit_bytes=56 * 1024 * 1024),
        cost_estimate=pl.CostEstimate(
            flops=PLANE * KC * 4 * BS**3,
            bytes_accessed=PLANE * KC * flat * 2,
            transcendentals=0,
        ),
        name="layer_" + ("upper" if layer else "lower"),
    )(scalars, a_blocks, own, zin, zout)


def per_device(a_blocks, a_cols, p_blocks, p_cols, coarse_owner):
    axes = ("slab", "grp")
    layers = lax.axis_size(axes)
    position = lax.axis_index(axes)
    depth_total = 2 * layers
    up = [(i, (i + 1) % layers) for i in range(layers)]
    down = [(j, i) for i, j in up]
    plane0 = p_blocks[:PLANE]
    plane1 = p_blocks[PLANE:]
    after = lax.ppermute(plane0, axes, down)
    before = lax.ppermute(plane1, axes, up)

    depth = 2 * position + lax.broadcasted_iota(jnp.int32, (2, PY, PX), 0)
    ypos = lax.broadcasted_iota(jnp.int32, (2, PY, PX), 1)
    xpos = lax.broadcasted_iota(jnp.int32, (2, PY, PX), 2)

    def locate(zz, yy, xx):
        return ((zz % depth_total * PY + yy % PY) * PX + xx % PX).reshape(2, PLANE)

    beside = [
        locate(depth, ypos, xpos),
        locate(depth, ypos, xpos - 1),
        locate(depth, ypos, xpos + 1),
        locate(depth, ypos - 1, xpos),
        locate(depth, ypos + 1, xpos),
    ]
    below, over = locate(depth - 1, ypos, xpos), locate(depth + 1, ypos, xpos)
    beside.append(jnp.stack([below[0], over[1]]))
    beside.append(jnp.stack([over[0], below[1]]))
    expected = jnp.stack(beside, axis=2)
    matches = a_cols.reshape(2, PLANE, 1, KC) == expected[..., None]
    chosen = jnp.sum(jnp.where(matches, jnp.arange(KC, dtype=jnp.int32), 0), axis=3)

    runs = p_cols[:PLANE].reshape(PY, PX)[:, 0] % RUNS
    down_in = (jnp.roll(runs, 1) == runs).astype(jnp.int32)
    up_in = (jnp.roll(runs, -1) == runs).astype(jnp.int32)

    def scalars(layer):
        owners = lax.dynamic_index_in_dim(
            coarse_owner, (position + layer) % layers, 0, keepdims=False
        )
        order = jnp.arange(AXY, dtype=jnp.int32)
        picked = jnp.sum(jnp.where(owners[None, :] == order[:, None], order[None, :], 0), axis=1)
        return jnp.concatenate([chosen[layer].reshape(-1), runs, down_in, up_in, picked])

    upper = layer_part(a_blocks, 1, scalars(1), plane1, after, plane0, 5, 6, BF16)
    arrived = lax.ppermute(upper, axes, up)
    lower = layer_part(a_blocks, 0, scalars(0), plane0, before, plane1, 6, 5, F32)
    summed = (lower + arrived.astype(F32)).astype(BF16)
    return lax.all_to_all(summed, "slab", split_axis=0, concat_axis=0, tiled=True)


def solution(mesh):
    return jax.shard_map(
        per_device,
        mesh=mesh,
        in_specs=(
            P(("slab", "grp"), None, None),
            P(("slab", "grp"), None),
            P(("slab", "grp"), None),
            P(("slab", "grp")),
            P(),
        ),
        out_specs=P(("slab", "grp"), None, None),
        check_vma=False,
    )
```

```python
import functools

import jax
import jax.numpy as jnp
from jax import lax
from jax.experimental import pallas as pl
from jax.experimental.pallas import tpu as pltpu
from jax.sharding import PartitionSpec as P

KC = 7
PX = 8
PY = 16
RUNS = 8
AXY = 32
PLANE = PX * PY
BS = 64
HALF = BS // 2
WIDE = 2 * BS
F32 = jnp.float32
BF16 = jnp.bfloat16


def swap(x):
    return pltpu.roll(x, BS, 1)


def spread(val, low, store):
    turned = swap(val)
    store[pl.ds(0, HALF, stride=2), :] = jnp.where(low, val, turned)
    store[pl.ds(1, HALF, stride=2), :] = jnp.where(low, turned, val)
    return turned


def align_kernel(scal, a_ref, p_ref, arel, prel, plhs, tmp, vtmp):
    step = pl.program_id(0)
    rows = a_ref.shape[1]
    low = lax.broadcasted_iota(jnp.int32, (HALF, WIDE), 1) < BS
    for k in range(KC):
        for i in range(HALF):
            tmp[k, i * rows : (i + 1) * rows, :] = a_ref[k, :, i * WIDE : (i + 1) * WIDE].astype(F32)
    for i in range(HALF):
        tmp[KC, i * rows : (i + 1) * rows, :] = p_ref[:, i * WIDE : (i + 1) * WIDE].astype(F32)
    for r in range(rows):
        for j in range(KC):
            k = scal[(step * rows + r) * KC + j]
            arel[j, r] = tmp[k, pl.ds(r, HALF, stride=rows), :].astype(BF16)
        val = tmp[KC, pl.ds(r, HALF, stride=rows), :]
        turned = spread(val, low, vtmp.at[r])
        prel[r] = vtmp[r].astype(BF16)
        plhs[r // 2, r % 2, 0] = val.astype(BF16)
        plhs[r // 2, r % 2, 1] = turned.astype(BF16)


def aligned(a_blocks, p_blocks, chosen):
    rows = 16
    count, flat = p_blocks.shape
    return pl.pallas_call(
        align_kernel,
        out_shape=(
            jax.ShapeDtypeStruct((KC, count, HALF, WIDE), BF16),
            jax.ShapeDtypeStruct((count, BS, WIDE), BF16),
            jax.ShapeDtypeStruct((count // 2, 2, 2, HALF, WIDE), BF16),
        ),
        grid_spec=pltpu.PrefetchScalarGridSpec(
            num_scalar_prefetch=1,
            grid=(count // rows,),
            in_specs=[
                pl.BlockSpec((KC, rows, flat), lambda s, _: (0, s, 0)),
                pl.BlockSpec((rows, flat), lambda s, _: (s, 0)),
            ],
            out_specs=(
                pl.BlockSpec((KC, rows, HALF, WIDE), lambda s, _: (0, s, 0, 0)),
                pl.BlockSpec((rows, BS, WIDE), lambda s, _: (s, 0, 0)),
                pl.BlockSpec((rows // 2, 2, 2, HALF, WIDE), lambda s, _: (s, 0, 0, 0, 0)),
            ),
            scratch_shapes=[
                pltpu.VMEM((KC + 1, rows * HALF, WIDE), F32),
                pltpu.VMEM((rows, BS, WIDE), F32),
            ],
        ),
        compiler_params=pltpu.CompilerParams(vmem_limit_bytes=32 * 1024 * 1024),
        cost_estimate=pl.CostEstimate(
            flops=0, bytes_accessed=5 * KC * count * flat, transcendentals=0
        ),
        name="align_blocks",
    )(chosen, a_blocks, p_blocks)


def layer_kernel(
    out_slot, zero_slot, scal, a_plane, a_down, a_up, a_zin, a_zout, p_own, p_out, zin_ref, plhs,
    out_ref, ptmp, vtmp, pin, carried, acc,
):
    y = pl.program_id(0)
    low = lax.broadcasted_iota(jnp.int32, (HALF, WIDE), 1) < BS
    low2 = lax.broadcasted_iota(jnp.int32, (BS, WIDE), 1) < BS

    @pl.when(y == 0)
    def _():
        rows = 16

        def some(n, _):
            part = zin_ref[pl.ds(pl.multiple_of(n * rows, rows), rows), :]
            for i in range(HALF):
                ptmp[i * rows : (i + 1) * rows, :] = part[:, i * WIDE : (i + 1) * WIDE].astype(F32)
            for r in range(rows):
                spread(ptmp[pl.ds(r, HALF, stride=rows), :], low, vtmp.at[r])
                pin[n * rows + r] = vtmp[r].astype(BF16)
            return 0

        lax.fori_loop(0, PLANE // rows, some, 0)

    def both(block):
        dup = block.astype(F32)
        top = jnp.where(low2, dup, 0.0)
        bottom = jnp.where(low2, 0.0, dup)
        return jnp.concatenate([top, bottom], axis=0).astype(BF16)

    above = lax.rem(y + 1, PY)
    below = lax.rem(y + PY - 1, PY)
    for x in range(PX):
        g = y * PX + x
        after, before = (x + 1) % PX, (x - 1) % PX
        lhs = jnp.concatenate(
            [a_plane[0, x], a_plane[1, after], a_plane[2, before], a_down[0, x], a_up[0, x]], axis=0
        )
        takers = (g, y * PX + after, y * PX + before, above * PX + x, below * PX + x)
        got = jnp.dot(lhs, both(p_own[x]), preferred_element_type=F32).astype(BF16)
        for j, f in enumerate(takers):
            carried[j, f] = got[j * HALF : (j + 1) * HALF]
        carried[5, g] = jnp.dot(a_zin[0, x], both(pin[g]), preferred_element_type=F32).astype(BF16)
        carried[6, g] = jnp.dot(a_zout[0, x], both(p_out[x]), preferred_element_type=F32).astype(
            BF16
        )

    @pl.when(y == pl.num_programs(0) - 1)
    def _():
        acc[...] = jnp.zeros_like(acc)

        def pair(a, b):
            return jnp.concatenate(
                [jnp.where(low, a, swap(b)), jnp.where(low, swap(a), b)], axis=0
            ).astype(BF16)

        def sum_row(y, _):
            run = scal[y]
            down_in = scal[PY + y] != 0
            up_in = scal[2 * PY + y] != 0
            zero = jnp.zeros((HALF, WIDE), F32)
            for c in range(PX // 2):
                parts = ([], [], [])
                for e in range(2):
                    f = y * PX + 2 * c + e
                    own, left, right, down, up, zin, zout = (
                        carried[j, f].astype(F32) for j in range(KC)
                    )
                    inner, outer = (right, left) if e == 0 else (left, right)
                    kept = (own + inner) + zin
                    kept = kept + jnp.where(down_in, down, zero) + jnp.where(up_in, up, zero)
                    down = jnp.where(down_in, zero, down)
                    up = jnp.where(up_in, zero, up)
                    parts[0].append(pair(kept, zout))
                    parts[1].append(pair(down, up))
                    parts[2].append(pair(outer, zero) if e == 0 else pair(zero, outer))
                at = (y * PX) // 2 + c
                lhs = plhs[at].reshape(2 * BS, WIDE)[:, :BS]
                q = c * RUNS + run
                for b in range(3):
                    acc[q, b] += lax.dot_general(
                        lhs,
                        jnp.concatenate(parts[b], axis=0),
                        (((0,), (0,)), ((), ())),
                        preferred_element_type=F32,
                    )
            return 0

        lax.fori_loop(0, PY, sum_row, 0)

        slots = ((0, out_slot), (3, 4), (1, 2))

        def write_row(o, _):
            q = scal[3 * PY + o]
            for b in range(3):
                even = acc[q, b, pl.ds(0, HALF, stride=2), :]
                odd = acc[q, b, pl.ds(1, HALF, stride=2), :]
                out_ref[o, slots[b][0]] = jnp.where(low, even, swap(odd)).astype(out_ref.dtype)
                out_ref[o, slots[b][1]] = jnp.where(low, swap(even), odd).astype(out_ref.dtype)
            out_ref[o, zero_slot] = jnp.zeros((HALF, WIDE), out_ref.dtype)
            return 0

        lax.fori_loop(0, AXY, write_row, 0)


def layer_part(blocks, layer, scalars, zin, out_slot, zero_slot, dtype):
    arel, prel, plhs = blocks
    flat = BS * BS
    base = layer * PY
    other = (1 - layer) * PY

    def taken(first, count, shift):
        return pl.BlockSpec(
            (count, PX, HALF, WIDE),
            lambda y, _: (first // count, base + lax.rem(y + PY + shift, PY), 0, 0),
        )

    return pl.pallas_call(
        functools.partial(layer_kernel, out_slot, zero_slot),
        out_shape=jax.ShapeDtypeStruct((AXY, KC, HALF, WIDE), dtype),
        grid_spec=pltpu.PrefetchScalarGridSpec(
            num_scalar_prefetch=1,
            grid=(PY,),
            in_specs=[
                taken(0, 3, 0),
                taken(3, 1, 1),
                taken(4, 1, -1),
                taken(5, 1, 0),
                taken(6, 1, 0),
                pl.BlockSpec((PX, BS, WIDE), lambda y, _: (base + y, 0, 0)),
                pl.BlockSpec((PX, BS, WIDE), lambda y, _: (other + y, 0, 0)),
                pl.BlockSpec((PLANE, flat), lambda y, _: (0, 0)),
                pl.BlockSpec((PLANE // 2, 2, 2, HALF, WIDE), lambda y, _: (layer, 0, 0, 0, 0)),
            ],
            out_specs=pl.BlockSpec((AXY, KC, HALF, WIDE), lambda y, _: (0, 0, 0, 0)),
            scratch_shapes=[
                pltpu.VMEM((16 * HALF, WIDE), F32),
                pltpu.VMEM((16, BS, WIDE), F32),
                pltpu.VMEM((PLANE, BS, WIDE), BF16),
                pltpu.VMEM((KC, PLANE, HALF, WIDE), BF16),
                pltpu.VMEM((AXY, 3, BS, WIDE), F32),
            ],
        ),
        compiler_params=pltpu.CompilerParams(vmem_limit_bytes=48 * 1024 * 1024),
        cost_estimate=pl.CostEstimate(
            flops=PLANE * KC * 4 * BS**3,
            bytes_accessed=PLANE * KC * flat * 2,
            transcendentals=0,
        ),
        name="layer_" + ("upper" if layer else "lower"),
    )(scalars, arel, arel, arel, arel, arel, prel, prel, zin, plhs)


def flat_kernel(in_ref, out_ref, tmp):
    rows = in_ref.shape[0]
    tmp[...] = in_ref[:, 0].astype(F32).reshape(rows * HALF, WIDE)
    for i in range(HALF):
        out_ref[0, :, i * WIDE : (i + 1) * WIDE] = tmp[pl.ds(i, rows, stride=HALF), :].astype(BF16)


def flattened(blocks):
    rows = blocks.shape[0]
    flat = BS * BS
    return pl.pallas_call(
        flat_kernel,
        out_shape=jax.ShapeDtypeStruct((KC, rows, flat), BF16),
        grid=(KC,),
        in_specs=[pl.BlockSpec((rows, 1, HALF, WIDE), lambda s: (0, s, 0, 0))],
        out_specs=pl.BlockSpec((1, rows, flat), lambda s: (s, 0, 0)),
        scratch_shapes=[pltpu.VMEM((rows * HALF, WIDE), F32)],
        name="flatten_rows",
    )(blocks)


def per_device(a_blocks, a_cols, p_blocks, p_cols, coarse_owner):
    axes = ("slab", "grp")
    layers = lax.axis_size(axes)
    position = lax.axis_index(axes)
    depth_total = 2 * layers
    up = [(i, (i + 1) % layers) for i in range(layers)]
    down = [(j, i) for i, j in up]
    plane0 = p_blocks[:PLANE]
    plane1 = p_blocks[PLANE:]
    after = lax.ppermute(plane0, axes, down)
    before = lax.ppermute(plane1, axes, up)
    after, before = lax.optimization_barrier((after, before))

    depth = 2 * position + lax.broadcasted_iota(jnp.int32, (2, PY, PX), 0)
    ypos = lax.broadcasted_iota(jnp.int32, (2, PY, PX), 1)
    xpos = lax.broadcasted_iota(jnp.int32, (2, PY, PX), 2)

    def locate(zz, yy, xx):
        return ((zz % depth_total * PY + yy % PY) * PX + xx % PX).reshape(2, PLANE)

    beside = [
        locate(depth, ypos, xpos),
        locate(depth, ypos, xpos - 1),
        locate(depth, ypos, xpos + 1),
        locate(depth, ypos - 1, xpos),
        locate(depth, ypos + 1, xpos),
    ]
    below, over = locate(depth - 1, ypos, xpos), locate(depth + 1, ypos, xpos)
    beside.append(jnp.stack([below[0], over[1]]))
    beside.append(jnp.stack([over[0], below[1]]))
    expected = jnp.stack(beside, axis=2)
    matches = a_cols.reshape(2, PLANE, 1, KC) == expected[..., None]
    chosen = jnp.sum(jnp.where(matches, jnp.arange(KC, dtype=jnp.int32), 0), axis=3)

    runs = p_cols[:PLANE].reshape(PY, PX)[:, 0] % RUNS
    down_in = (jnp.roll(runs, 1) == runs).astype(jnp.int32)
    up_in = (jnp.roll(runs, -1) == runs).astype(jnp.int32)

    def scalars(layer):
        owners = lax.dynamic_index_in_dim(
            coarse_owner, (position + layer) % layers, 0, keepdims=False
        )
        order = jnp.arange(AXY, dtype=jnp.int32)
        picked = jnp.sum(jnp.where(owners[None, :] == order[:, None], order[None, :], 0), axis=1)
        return jnp.concatenate([runs, down_in, up_in, picked])

    blocks = aligned(jnp.transpose(a_blocks, (1, 0, 2)), p_blocks, chosen.reshape(-1))
    upper = layer_part(blocks, 1, scalars(1), after, 5, 6, BF16)
    arrived = lax.ppermute(upper, axes, up)
    lower = layer_part(blocks, 0, scalars(0), before, 6, 5, F32)
    summed = (lower + arrived.astype(F32)).astype(BF16)
    placed = lax.all_to_all(summed, "slab", split_axis=0, concat_axis=0, tiled=True)
    return jnp.transpose(flattened(placed), (1, 0, 2))


def solution(mesh):
    return jax.shard_map(
        per_device,
        mesh=mesh,
        in_specs=(
            P(("slab", "grp"), None, None),
            P(("slab", "grp"), None),
            P(("slab", "grp"), None),
            P(("slab", "grp")),
            P(),
        ),
        out_specs=P(("slab", "grp"), None, None),
        check_vma=False,
    )
```

```python
import functools

import jax
import jax.numpy as jnp
from jax import lax
from jax.experimental import pallas as pl
from jax.experimental.pallas import tpu as pltpu
from jax.sharding import PartitionSpec as P

KC = 7
PX = 8
PY = 16
RUNS = 8
AXY = 32
PLANE = PX * PY
BS = 64
HALF = BS // 2
WIDE = 2 * BS
F32 = jnp.float32
BF16 = jnp.bfloat16
NEAR = 5
PITCH = 17


def swap(x):
    return pltpu.roll(x, BS, 1)


def spread(val, low, store):
    turned = swap(val)
    store[pl.ds(0, HALF, stride=2), :] = jnp.where(low, val, turned)
    store[pl.ds(1, HALF, stride=2), :] = jnp.where(low, turned, val)
    return turned


def align_kernel(scal, a_ref, p_ref, near, far, prel, plhs, tmp, vtmp):
    step = pl.program_id(0)
    rows = a_ref.shape[1]
    low = lax.broadcasted_iota(jnp.int32, (HALF, WIDE), 1) < BS
    for k in range(KC):
        for i in range(HALF):
            tmp[k, i * PITCH : i * PITCH + rows, :] = a_ref[k, :, i * WIDE : (i + 1) * WIDE].astype(F32)
    for i in range(HALF):
        tmp[KC, i * PITCH : i * PITCH + rows, :] = p_ref[:, i * WIDE : (i + 1) * WIDE].astype(F32)
    for r in range(rows):
        for j in range(KC):
            k = scal[(step * rows + r) * KC + j]
            block = tmp[k, pl.ds(r, HALF, stride=PITCH), :].astype(BF16)
            if j < NEAR:
                near[j, r] = block
            else:
                far[j - NEAR, r] = block
        val = tmp[KC, pl.ds(r, HALF, stride=PITCH), :]
        turned = spread(val, low, vtmp.at[r])
        prel[r] = vtmp[r].astype(BF16)
        plhs[r // 2, r % 2, 0] = val.astype(BF16)
        plhs[r // 2, r % 2, 1] = turned.astype(BF16)


def aligned(a_blocks, p_blocks, chosen):
    rows = 16
    count, flat = p_blocks.shape
    return pl.pallas_call(
        align_kernel,
        out_shape=(
            jax.ShapeDtypeStruct((NEAR, count, HALF, WIDE), BF16),
            jax.ShapeDtypeStruct((KC - NEAR, count, HALF, WIDE), BF16),
            jax.ShapeDtypeStruct((count, BS, WIDE), BF16),
            jax.ShapeDtypeStruct((count // 2, 2, 2, HALF, WIDE), BF16),
        ),
        grid_spec=pltpu.PrefetchScalarGridSpec(
            num_scalar_prefetch=1,
            grid=(count // rows,),
            in_specs=[
                pl.BlockSpec((KC, rows, flat), lambda s, _: (0, s, 0)),
                pl.BlockSpec((rows, flat), lambda s, _: (s, 0)),
            ],
            out_specs=(
                pl.BlockSpec((NEAR, rows, HALF, WIDE), lambda s, _: (0, s, 0, 0)),
                pl.BlockSpec((KC - NEAR, rows, HALF, WIDE), lambda s, _: (0, s, 0, 0)),
                pl.BlockSpec((rows, BS, WIDE), lambda s, _: (s, 0, 0)),
                pl.BlockSpec((rows // 2, 2, 2, HALF, WIDE), lambda s, _: (s, 0, 0, 0, 0)),
            ),
            scratch_shapes=[
                pltpu.VMEM((KC + 1, PITCH * HALF, WIDE), F32),
                pltpu.VMEM((rows, BS, WIDE), F32),
            ],
        ),
        compiler_params=pltpu.CompilerParams(vmem_limit_bytes=32 * 1024 * 1024),
        cost_estimate=pl.CostEstimate(
            flops=0, bytes_accessed=5 * KC * count * flat, transcendentals=0
        ),
        name="align_blocks",
    )(chosen, a_blocks, p_blocks)


def lane_masks():
    low = lax.broadcasted_iota(jnp.int32, (HALF, WIDE), 1) < BS
    low2 = lax.broadcasted_iota(jnp.int32, (BS, WIDE), 1) < BS
    return low, low2


def both(block, low2):
    dup = block.astype(F32)
    top = jnp.where(low2, dup, 0.0)
    bottom = jnp.where(low2, 0.0, dup)
    return jnp.concatenate([top, bottom], axis=0).astype(BF16)


def pair(a, b, low):
    return jnp.concatenate(
        [jnp.where(low, a, swap(b)), jnp.where(low, swap(a), b)], axis=0
    ).astype(BF16)


def add_product(acc, plhs, at, q, parts):
    lhs = plhs[at].reshape(2 * BS, WIDE)[:, :BS]
    for b, part in enumerate(parts):
        acc[q, b] += lax.dot_general(
            lhs,
            jnp.concatenate(part, axis=0),
            (((0,), (0,)), ((), ())),
            preferred_element_type=F32,
        )


def write_rows(scal, acc, out_ref, low):
    def write_row(o, _):
        q = scal[3 * PY + o]
        for b in range(2):
            even = acc[q, b, pl.ds(0, HALF, stride=2), :]
            odd = acc[q, b, pl.ds(1, HALF, stride=2), :]
            out_ref[o, 2 * b] = jnp.where(low, even, swap(odd)).astype(out_ref.dtype)
            if b == 0:
                out_ref[o, 1] = jnp.where(low, swap(even), odd).astype(out_ref.dtype)
        return 0

    lax.fori_loop(0, AXY, write_row, 0)


def outer_x(x):
    return (x - 1) % PX if x % 2 == 0 else (x + 1) % PX


def far_kernel(scal, blocks, p_own, p_out, plhs, out_ref, carried, acc):
    low, low2 = lane_masks()

    def carry_row(y, _):
        for x in range(PX):
            g = y * PX + x
            f = y * PX + outer_x(x)
            carried[0, f] = jnp.dot(blocks[0, f], both(p_own[g], low2), preferred_element_type=F32)
            carried[1, g] = jnp.dot(blocks[1, g], both(p_out[g], low2), preferred_element_type=F32)
        return 0

    lax.fori_loop(0, PY, carry_row, 0)
    acc[...] = jnp.zeros_like(acc)

    def sum_row(y, _):
        run = scal[y]
        zero = jnp.zeros((HALF, WIDE), F32)
        for c in range(PX // 2):
            parts = ([], [])
            for e in range(2):
                f = y * PX + 2 * c + e
                side = carried[0, f]
                parts[0].append(pair(side, zero, low) if e == 0 else pair(zero, side, low))
                parts[1].append(pair(carried[1, f], zero, low))
            add_product(acc, plhs, (y * PX) // 2 + c, c * RUNS + run, parts)
        return 0

    lax.fori_loop(0, PY, sum_row, 0)
    write_rows(scal, acc, out_ref, low)


def near_kernel(scal, blocks, p_own, zin_ref, plhs, out_ref, ptmp, vtmp, pin, carried, acc):
    low, low2 = lane_masks()
    rows = 16

    def some(n, _):
        part = zin_ref[pl.ds(pl.multiple_of(n * rows, rows), rows), :]
        for i in range(HALF):
            ptmp[i * PITCH : i * PITCH + rows, :] = part[:, i * WIDE : (i + 1) * WIDE].astype(F32)
        for r in range(rows):
            spread(ptmp[pl.ds(r, HALF, stride=PITCH), :], low, vtmp.at[r])
            pin[n * rows + r] = vtmp[r].astype(BF16)
        return 0

    lax.fori_loop(0, PLANE // rows, some, 0)

    def carry_row(y, _):
        above = lax.rem(y + 1, PY)
        below = lax.rem(y + PY - 1, PY)
        for x in range(PX):
            g = y * PX + x
            takers = (g, y * PX + (x ^ 1), above * PX + x, below * PX + x)
            lhs = jnp.concatenate([blocks[j, f] for j, f in enumerate(takers)], axis=0)
            got = jnp.dot(lhs, both(p_own[g], low2), preferred_element_type=F32).astype(BF16)
            for j, f in enumerate(takers):
                carried[j, f] = got[j * HALF : (j + 1) * HALF]
            carried[4, g] = jnp.dot(
                blocks[4, g], both(pin[g], low2), preferred_element_type=F32
            ).astype(BF16)
        return 0

    lax.fori_loop(0, PY, carry_row, 0)
    acc[...] = jnp.zeros_like(acc)

    def sum_row(y, _):
        run = scal[y]
        down_in = scal[PY + y] != 0
        up_in = scal[2 * PY + y] != 0
        zero = jnp.zeros((HALF, WIDE), F32)
        for c in range(PX // 2):
            parts = ([], [])
            for e in range(2):
                f = y * PX + 2 * c + e
                own, inner, down, up, zin = (carried[j, f].astype(F32) for j in range(NEAR))
                kept = (own + inner) + zin
                kept = kept + jnp.where(down_in, down, zero) + jnp.where(up_in, up, zero)
                down = jnp.where(down_in, zero, down)
                up = jnp.where(up_in, zero, up)
                parts[0].append(pair(down, up, low))
                parts[1].append(pair(kept, zero, low))
            add_product(acc, plhs, (y * PX) // 2 + c, c * RUNS + run, parts)
        return 0

    lax.fori_loop(0, PY, sum_row, 0)
    write_rows(scal, acc, out_ref, low)


def layer_part(kernel, name, layer, dtype, scalars, blocks, prel, plhs, zin=None):
    count = blocks.shape[0]
    flat = BS * BS
    plane = pl.BlockSpec((PLANE, BS, WIDE), lambda s, _: (layer, 0, 0))
    if zin is None:
        last = (pl.BlockSpec((PLANE, BS, WIDE), lambda s, _: (1 - layer, 0, 0)), prel)
        scratch = [pltpu.VMEM((KC - NEAR, PLANE, HALF, WIDE), F32)]
    else:
        last = (pl.BlockSpec((PLANE, flat), lambda s, _: (0, 0)), zin)
        scratch = [
            pltpu.VMEM((PITCH * HALF, WIDE), F32),
            pltpu.VMEM((16, BS, WIDE), F32),
            pltpu.VMEM((PLANE, BS, WIDE), BF16),
            pltpu.VMEM((NEAR, PLANE, HALF, WIDE), BF16),
        ]
    return pl.pallas_call(
        kernel,
        out_shape=jax.ShapeDtypeStruct((AXY, 3, HALF, WIDE), dtype),
        grid_spec=pltpu.PrefetchScalarGridSpec(
            num_scalar_prefetch=1,
            grid=(1,),
            in_specs=[
                pl.BlockSpec((count, PLANE, HALF, WIDE), lambda s, _: (0, layer, 0, 0)),
                plane,
                last[0],
                pl.BlockSpec((PLANE // 2, 2, 2, HALF, WIDE), lambda s, _: (layer, 0, 0, 0, 0)),
            ],
            out_specs=pl.BlockSpec((AXY, 3, HALF, WIDE), lambda s, _: (0, 0, 0, 0)),
            scratch_shapes=scratch + [pltpu.VMEM((AXY, 2, BS, WIDE), F32)],
        ),
        compiler_params=pltpu.CompilerParams(vmem_limit_bytes=44 * 1024 * 1024),
        cost_estimate=pl.CostEstimate(
            flops=PLANE * count * 64 * BS**3,
            bytes_accessed=PLANE * count * flat * 2,
            transcendentals=0,
        ),
        name=name + ("_upper" if layer else "_lower"),
    )(scalars, blocks, prel, last[1], plhs)


def flat_kernel(in_ref, *refs):
    out_ref, tmp = refs[-2:]
    rows = in_ref.shape[0]
    for o in range(rows):
        tmp[o * (HALF + 1) : o * (HALF + 1) + HALF] = in_ref[o, 0].astype(F32)
    for i in range(HALF):
        out_ref[0, :, i * WIDE : (i + 1) * WIDE] = tmp[pl.ds(i, rows, stride=HALF + 1), :].astype(BF16)


def flattened(blocks, slot_of_part, into=None):
    rows, parts = blocks.shape[:2]
    flat = BS * BS
    kept = [] if into is None else [into]
    return pl.pallas_call(
        flat_kernel,
        out_shape=jax.ShapeDtypeStruct((KC, rows, flat), BF16),
        grid=(parts,),
        in_specs=[pl.BlockSpec((rows, 1, HALF, WIDE), lambda s: (0, s, 0, 0))]
        + [pl.BlockSpec(memory_space=pl.ANY) for _ in kept],
        out_specs=pl.BlockSpec((1, rows, flat), lambda s: (slot_of_part(s), 0, 0)),
        scratch_shapes=[pltpu.VMEM((rows * (HALF + 1), WIDE), F32)],
        input_output_aliases={1: 0} if kept else {},
        name="flatten_" + ("near" if kept else "far"),
    )(blocks, *kept)


def per_device(a_blocks, a_cols, p_blocks, p_cols, coarse_owner):
    axes = ("slab", "grp")
    layers = lax.axis_size(axes)
    position = lax.axis_index(axes)
    depth_total = 2 * layers
    up = [(i, (i + 1) % layers) for i in range(layers)]
    down = [(j, i) for i, j in up]
    plane0 = p_blocks[:PLANE]
    plane1 = p_blocks[PLANE:]
    after = lax.ppermute(plane0, axes, down)
    before = lax.ppermute(plane1, axes, up)
    after, before = lax.optimization_barrier((after, before))

    depth = 2 * position + lax.broadcasted_iota(jnp.int32, (2, PY, PX), 0)
    ypos = lax.broadcasted_iota(jnp.int32, (2, PY, PX), 1)
    xpos = lax.broadcasted_iota(jnp.int32, (2, PY, PX), 2)

    def locate(zz, yy, xx):
        return ((zz % depth_total * PY + yy % PY) * PX + xx % PX).reshape(2, PLANE)

    beside = [
        locate(depth, ypos, xpos),
        locate(depth, ypos, xpos + 1 - 2 * (xpos % 2)),
        locate(depth, ypos - 1, xpos),
        locate(depth, ypos + 1, xpos),
    ]
    below, over = locate(depth - 1, ypos, xpos), locate(depth + 1, ypos, xpos)
    beside.append(jnp.stack([below[0], over[1]]))
    beside.append(locate(depth, ypos, xpos - 1 + 2 * (xpos % 2)))
    beside.append(jnp.stack([over[0], below[1]]))
    expected = jnp.stack(beside, axis=2)
    matches = a_cols.reshape(2, PLANE, 1, KC) == expected[..., None]
    chosen = jnp.sum(jnp.where(matches, jnp.arange(KC, dtype=jnp.int32), 0), axis=3)

    runs = p_cols[:PLANE].reshape(PY, PX)[:, 0] % RUNS
    down_in = (jnp.roll(runs, 1) == runs).astype(jnp.int32)
    up_in = (jnp.roll(runs, -1) == runs).astype(jnp.int32)

    def scalars(layer):
        owners = lax.dynamic_index_in_dim(
            coarse_owner, (position + layer) % layers, 0, keepdims=False
        )
        order = jnp.arange(AXY, dtype=jnp.int32)
        picked = jnp.sum(jnp.where(owners[None, :] == order[:, None], order[None, :], 0), axis=1)
        return jnp.concatenate([runs, down_in, up_in, picked])

    near, far, prel, plhs = aligned(jnp.transpose(a_blocks, (1, 0, 2)), p_blocks, chosen.reshape(-1))
    scal = (scalars(0), scalars(1))

    def exchanged(rows):
        return lax.all_to_all(rows, "slab", split_axis=0, concat_axis=0, tiled=True)

    upper = layer_part(far_kernel, "far", 1, BF16, scal[1], far, prel, plhs)
    arrived = lax.ppermute(upper, axes, up)
    lower = layer_part(far_kernel, "far", 0, F32, scal[0], far, prel, plhs)
    sides = (lower[:, :2] + arrived[:, :2].astype(F32)).astype(BF16)
    far_rows = jnp.concatenate([sides, arrived[:, 2:], lower[:, 2:].astype(BF16)], axis=1)
    far_rows, near = lax.optimization_barrier((far_rows, near))
    far_rows = exchanged(far_rows)

    upper = layer_part(near_kernel, "near", 1, BF16, scal[1], near, prel, plhs, after)
    arrived = lax.ppermute(upper, axes, up)
    lower = layer_part(near_kernel, "near", 0, F32, scal[0], near, prel, plhs, before)
    near_rows = exchanged((lower + arrived.astype(F32)).astype(BF16))

    flat = flattened(far_rows, lambda s: jnp.where(s < 2, s + 1, s + 3))
    flat = flattened(near_rows, lambda s: jnp.where(s < 2, s + 3, 0), flat)
    return jnp.transpose(flat, (1, 0, 2))


def solution(mesh):
    return jax.shard_map(
        per_device,
        mesh=mesh,
        in_specs=(
            P(("slab", "grp"), None, None),
            P(("slab", "grp"), None),
            P(("slab", "grp"), None),
            P(("slab", "grp")),
            P(),
        ),
        out_specs=P(("slab", "grp"), None, None),
        check_vma=False,
    )
```

```python
import functools

import jax
import jax.numpy as jnp
from jax import lax
from jax.experimental import pallas as pl
from jax.experimental.pallas import tpu as pltpu
from jax.sharding import PartitionSpec as P

KC = 7
PX = 8
PY = 16
RUNS = 8
AXY = 32
PLANE = PX * PY
BS = 64
HALF = BS // 2
WIDE = 2 * BS
F32 = jnp.float32
BF16 = jnp.bfloat16
NEAR = 5
PITCH = 17


def swap(x):
    return pltpu.roll(x, BS, 1)


def spread(val, low, store):
    turned = swap(val)
    store[pl.ds(0, HALF, stride=2), :] = jnp.where(low, val, turned)
    store[pl.ds(1, HALF, stride=2), :] = jnp.where(low, turned, val)
    return turned


def align_kernel(scal, a_ref, p_ref, near, far, prel, plhs, tmp, vtmp):
    step = pl.program_id(0)
    rows = a_ref.shape[1]
    low = lax.broadcasted_iota(jnp.int32, (HALF, WIDE), 1) < BS
    for k in range(KC):
        for i in range(HALF):
            tmp[k, i * PITCH : i * PITCH + rows, :] = a_ref[k, :, i * WIDE : (i + 1) * WIDE].astype(F32)
    for i in range(HALF):
        tmp[KC, i * PITCH : i * PITCH + rows, :] = p_ref[:, i * WIDE : (i + 1) * WIDE].astype(F32)
    for r in range(rows):
        for j in range(KC):
            k = scal[(step * rows + r) * KC + j]
            block = tmp[k, pl.ds(r, HALF, stride=PITCH), :].astype(BF16)
            if j < NEAR:
                near[j, r] = block
            else:
                far[j - NEAR, r] = block
        val = tmp[KC, pl.ds(r, HALF, stride=PITCH), :]
        turned = spread(val, low, vtmp.at[r])
        prel[r] = vtmp[r].astype(BF16)
        plhs[r // 2, r % 2, 0] = val.astype(BF16)
        plhs[r // 2, r % 2, 1] = turned.astype(BF16)


def aligned(a_blocks, p_blocks, chosen):
    rows = 16
    count, flat = p_blocks.shape
    return pl.pallas_call(
        align_kernel,
        out_shape=(
            jax.ShapeDtypeStruct((NEAR, count, HALF, WIDE), BF16),
            jax.ShapeDtypeStruct((KC - NEAR, count, HALF, WIDE), BF16),
            jax.ShapeDtypeStruct((count, BS, WIDE), BF16),
            jax.ShapeDtypeStruct((count // 2, 2, 2, HALF, WIDE), BF16),
        ),
        grid_spec=pltpu.PrefetchScalarGridSpec(
            num_scalar_prefetch=1,
            grid=(count // rows,),
            in_specs=[
                pl.BlockSpec((KC, rows, flat), lambda s, _: (0, s, 0)),
                pl.BlockSpec((rows, flat), lambda s, _: (s, 0)),
            ],
            out_specs=(
                pl.BlockSpec((NEAR, rows, HALF, WIDE), lambda s, _: (0, s, 0, 0)),
                pl.BlockSpec((KC - NEAR, rows, HALF, WIDE), lambda s, _: (0, s, 0, 0)),
                pl.BlockSpec((rows, BS, WIDE), lambda s, _: (s, 0, 0)),
                pl.BlockSpec((rows // 2, 2, 2, HALF, WIDE), lambda s, _: (s, 0, 0, 0, 0)),
            ),
            scratch_shapes=[
                pltpu.VMEM((KC + 1, PITCH * HALF, WIDE), F32),
                pltpu.VMEM((rows, BS, WIDE), F32),
            ],
        ),
        compiler_params=pltpu.CompilerParams(vmem_limit_bytes=32 * 1024 * 1024),
        cost_estimate=pl.CostEstimate(
            flops=0, bytes_accessed=5 * KC * count * flat, transcendentals=0
        ),
        name="align_blocks",
    )(chosen, a_blocks, p_blocks)


def lane_masks():
    low = lax.broadcasted_iota(jnp.int32, (HALF, WIDE), 1) < BS
    low2 = lax.broadcasted_iota(jnp.int32, (BS, WIDE), 1) < BS
    return low, low2


def both(block, low2):
    dup = block.astype(F32)
    top = jnp.where(low2, dup, 0.0)
    bottom = jnp.where(low2, 0.0, dup)
    return jnp.concatenate([top, bottom], axis=0).astype(BF16)


def pair(a, b, low):
    return jnp.concatenate(
        [jnp.where(low, a, swap(b)), jnp.where(low, swap(a), b)], axis=0
    ).astype(BF16)


def add_product(acc, plhs, at, q, parts):
    lhs = plhs[at].reshape(2 * BS, WIDE)[:, :BS]
    for b, part in enumerate(parts):
        acc[q, b] += lax.dot_general(
            lhs,
            jnp.concatenate(part, axis=0),
            (((0,), (0,)), ((), ())),
            preferred_element_type=F32,
        )


def write_rows(scal, acc, out_ref, low):
    def write_row(o, _):
        q = scal[3 * PY + o]
        for b in range(2):
            even = acc[q, b, pl.ds(0, HALF, stride=2), :]
            odd = acc[q, b, pl.ds(1, HALF, stride=2), :]
            out_ref[o, 2 * b] = jnp.where(low, even, swap(odd)).astype(out_ref.dtype)
            if b == 0:
                out_ref[o, 1] = jnp.where(low, swap(even), odd).astype(out_ref.dtype)
        return 0

    lax.fori_loop(0, AXY, write_row, 0)


def outer_x(x):
    return (x - 1) % PX if x % 2 == 0 else (x + 1) % PX


def far_kernel(scal, blocks, p_own, p_out, plhs, out_ref, carried, acc):
    low, low2 = lane_masks()

    def carry_row(y, _):
        for x in range(PX):
            g = y * PX + x
            f = y * PX + outer_x(x)
            carried[0, f] = jnp.dot(blocks[0, f], both(p_own[g], low2), preferred_element_type=F32)
            carried[1, g] = jnp.dot(blocks[1, g], both(p_out[g], low2), preferred_element_type=F32)
        return 0

    lax.fori_loop(0, PY, carry_row, 0)
    acc[...] = jnp.zeros_like(acc)

    def sum_row(y, _):
        run = scal[y]
        zero = jnp.zeros((HALF, WIDE), F32)
        for c in range(PX // 2):
            parts = ([], [])
            for e in range(2):
                f = y * PX + 2 * c + e
                side = carried[0, f]
                parts[0].append(pair(side, zero, low) if e == 0 else pair(zero, side, low))
                parts[1].append(pair(carried[1, f], zero, low))
            add_product(acc, plhs, (y * PX) // 2 + c, c * RUNS + run, parts)
        return 0

    lax.fori_loop(0, PY, sum_row, 0)
    write_rows(scal, acc, out_ref, low)


def near_kernel(scal, blocks, p_own, zin_ref, plhs, out_ref, ptmp, vtmp, pin, carried, acc):
    low, low2 = lane_masks()
    rows = 16

    def some(n, _):
        part = zin_ref[pl.ds(pl.multiple_of(n * rows, rows), rows), :]
        for i in range(HALF):
            ptmp[i * PITCH : i * PITCH + rows, :] = part[:, i * WIDE : (i + 1) * WIDE].astype(F32)
        for r in range(rows):
            spread(ptmp[pl.ds(r, HALF, stride=PITCH), :], low, vtmp.at[r])
            pin[n * rows + r] = vtmp[r].astype(BF16)
        return 0

    lax.fori_loop(0, PLANE // rows, some, 0)

    def carry_row(y, _):
        above = lax.rem(y + 1, PY)
        below = lax.rem(y + PY - 1, PY)
        for x in range(PX):
            g = y * PX + x
            takers = (g, y * PX + (x ^ 1), above * PX + x, below * PX + x)
            lhs = jnp.concatenate([blocks[j, f] for j, f in enumerate(takers)], axis=0)
            got = jnp.dot(lhs, both(p_own[g], low2), preferred_element_type=F32).astype(BF16)
            for j, f in enumerate(takers):
                carried[j, f] = got[j * HALF : (j + 1) * HALF]
            carried[4, g] = jnp.dot(
                blocks[4, g], both(pin[g], low2), preferred_element_type=F32
            ).astype(BF16)
        return 0

    lax.fori_loop(0, PY, carry_row, 0)
    acc[...] = jnp.zeros_like(acc)

    def sum_row(y, _):
        run = scal[y]
        down_in = scal[PY + y] != 0
        up_in = scal[2 * PY + y] != 0
        zero = jnp.zeros((HALF, WIDE), F32)
        for c in range(PX // 2):
            parts = ([], [])
            for e in range(2):
                f = y * PX + 2 * c + e
                own, inner, down, up, zin = (carried[j, f].astype(F32) for j in range(NEAR))
                kept = (own + inner) + zin
                kept = kept + jnp.where(down_in, down, zero) + jnp.where(up_in, up, zero)
                down = jnp.where(down_in, zero, down)
                up = jnp.where(up_in, zero, up)
                parts[0].append(pair(down, up, low))
                parts[1].append(pair(kept, zero, low))
            add_product(acc, plhs, (y * PX) // 2 + c, c * RUNS + run, parts)
        return 0

    lax.fori_loop(0, PY, sum_row, 0)
    write_rows(scal, acc, out_ref, low)


def layer_part(kernel, name, layer, dtype, scalars, blocks, prel, plhs, zin=None):
    count = blocks.shape[0]
    flat = BS * BS
    plane = pl.BlockSpec((PLANE, BS, WIDE), lambda s, _: (layer, 0, 0))
    if zin is None:
        last = (pl.BlockSpec((PLANE, BS, WIDE), lambda s, _: (1 - layer, 0, 0)), prel)
        scratch = [pltpu.VMEM((KC - NEAR, PLANE, HALF, WIDE), F32)]
    else:
        last = (pl.BlockSpec((PLANE, flat), lambda s, _: (0, 0)), zin)
        scratch = [
            pltpu.VMEM((PITCH * HALF, WIDE), F32),
            pltpu.VMEM((16, BS, WIDE), F32),
            pltpu.VMEM((PLANE, BS, WIDE), BF16),
            pltpu.VMEM((NEAR, PLANE, HALF, WIDE), BF16),
        ]
    return pl.pallas_call(
        kernel,
        out_shape=jax.ShapeDtypeStruct((AXY, 3, HALF, WIDE), dtype),
        grid_spec=pltpu.PrefetchScalarGridSpec(
            num_scalar_prefetch=1,
            grid=(1,),
            in_specs=[
                pl.BlockSpec((count, PLANE, HALF, WIDE), lambda s, _: (0, layer, 0, 0)),
                plane,
                last[0],
                pl.BlockSpec((PLANE // 2, 2, 2, HALF, WIDE), lambda s, _: (layer, 0, 0, 0, 0)),
            ],
            out_specs=pl.BlockSpec((AXY, 3, HALF, WIDE), lambda s, _: (0, 0, 0, 0)),
            scratch_shapes=scratch + [pltpu.VMEM((AXY, 2, BS, WIDE), F32)],
        ),
        compiler_params=pltpu.CompilerParams(vmem_limit_bytes=44 * 1024 * 1024),
        cost_estimate=pl.CostEstimate(
            flops=PLANE * count * 64 * BS**3,
            bytes_accessed=PLANE * count * flat * 2,
            transcendentals=0,
        ),
        name=name + ("_upper" if layer else "_lower"),
    )(scalars, blocks, prel, last[1], plhs)


def flat_kernel(in_ref, *refs):
    out_ref, tmp = refs[-2:]
    rows = in_ref.shape[0]
    for o in range(rows):
        tmp[o * (HALF + 1) : o * (HALF + 1) + HALF] = in_ref[o, 0].astype(F32)
    for i in range(HALF):
        out_ref[0, :, i * WIDE : (i + 1) * WIDE] = tmp[pl.ds(i, rows, stride=HALF + 1), :].astype(BF16)


def flattened(blocks, slot_of_part, into=None):
    rows, parts = blocks.shape[:2]
    flat = BS * BS
    kept = [] if into is None else [into]
    return pl.pallas_call(
        flat_kernel,
        out_shape=jax.ShapeDtypeStruct((KC, rows, flat), BF16),
        grid=(parts,),
        in_specs=[pl.BlockSpec((rows, 1, HALF, WIDE), lambda s: (0, s, 0, 0))]
        + [pl.BlockSpec(memory_space=pl.ANY) for _ in kept],
        out_specs=pl.BlockSpec((1, rows, flat), lambda s: (slot_of_part(s), 0, 0)),
        scratch_shapes=[pltpu.VMEM((rows * (HALF + 1), WIDE), F32)],
        input_output_aliases={1: 0} if kept else {},
        name="flatten_" + ("near" if kept else "far"),
    )(blocks, *kept)


def per_device(a_blocks, a_cols, p_blocks, p_cols, coarse_owner):
    axes = ("slab", "grp")
    layers = lax.axis_size(axes)
    position = lax.axis_index(axes)
    depth_total = 2 * layers
    up = [(i, (i + 1) % layers) for i in range(layers)]
    down = [(j, i) for i, j in up]
    plane0 = p_blocks[:PLANE]
    plane1 = p_blocks[PLANE:]
    after = lax.ppermute(plane0, axes, down)
    before = lax.ppermute(plane1, axes, up)

    depth = 2 * position + lax.broadcasted_iota(jnp.int32, (2, PY, PX), 0)
    ypos = lax.broadcasted_iota(jnp.int32, (2, PY, PX), 1)
    xpos = lax.broadcasted_iota(jnp.int32, (2, PY, PX), 2)

    def locate(zz, yy, xx):
        return ((zz % depth_total * PY + yy % PY) * PX + xx % PX).reshape(2, PLANE)

    beside = [
        locate(depth, ypos, xpos),
        locate(depth, ypos, xpos + 1 - 2 * (xpos % 2)),
        locate(depth, ypos - 1, xpos),
        locate(depth, ypos + 1, xpos),
    ]
    below, over = locate(depth - 1, ypos, xpos), locate(depth + 1, ypos, xpos)
    beside.append(jnp.stack([below[0], over[1]]))
    beside.append(locate(depth, ypos, xpos - 1 + 2 * (xpos % 2)))
    beside.append(jnp.stack([over[0], below[1]]))
    expected = jnp.stack(beside, axis=2)
    matches = a_cols.reshape(2, PLANE, 1, KC) == expected[..., None]
    chosen = jnp.sum(jnp.where(matches, jnp.arange(KC, dtype=jnp.int32), 0), axis=3)

    runs = p_cols[:PLANE].reshape(PY, PX)[:, 0] % RUNS
    down_in = (jnp.roll(runs, 1) == runs).astype(jnp.int32)
    up_in = (jnp.roll(runs, -1) == runs).astype(jnp.int32)

    def scalars(layer):
        owners = lax.dynamic_index_in_dim(
            coarse_owner, (position + layer) % layers, 0, keepdims=False
        )
        order = jnp.arange(AXY, dtype=jnp.int32)
        picked = jnp.sum(jnp.where(owners[None, :] == order[:, None], order[None, :], 0), axis=1)
        return jnp.concatenate([runs, down_in, up_in, picked])

    near, far, prel, plhs = aligned(jnp.transpose(a_blocks, (1, 0, 2)), p_blocks, chosen.reshape(-1))
    scal = (scalars(0), scalars(1))
    after, before, far = lax.optimization_barrier((after, before, far))

    def exchanged(rows):
        return lax.all_to_all(rows, "slab", split_axis=0, concat_axis=0, tiled=True)

    upper = layer_part(far_kernel, "far", 1, BF16, scal[1], far, prel, plhs)
    arrived = lax.ppermute(upper, axes, up)
    lower = layer_part(far_kernel, "far", 0, F32, scal[0], far, prel, plhs)
    sides = (lower[:, :2] + arrived[:, :2].astype(F32)).astype(BF16)
    far_rows = jnp.concatenate([sides, arrived[:, 2:], lower[:, 2:].astype(BF16)], axis=1)
    far_rows, near = lax.optimization_barrier((far_rows, near))
    far_rows = exchanged(far_rows)

    upper = layer_part(near_kernel, "near", 1, BF16, scal[1], near, prel, plhs, after)
    arrived = lax.ppermute(upper, axes, up)
    lower = layer_part(near_kernel, "near", 0, F32, scal[0], near, prel, plhs, before)
    near_rows = exchanged((lower + arrived.astype(F32)).astype(BF16))

    flat = flattened(far_rows, lambda s: jnp.where(s < 2, s + 1, s + 3))
    flat = flattened(near_rows, lambda s: jnp.where(s < 2, s + 3, 0), flat)
    return jnp.transpose(flat, (1, 0, 2))


def solution(mesh):
    return jax.shard_map(
        per_device,
        mesh=mesh,
        in_specs=(
            P(("slab", "grp"), None, None),
            P(("slab", "grp"), None),
            P(("slab", "grp"), None),
            P(("slab", "grp")),
            P(),
        ),
        out_specs=P(("slab", "grp"), None, None),
        check_vma=False,
    )
```

```python
import functools

import jax
import jax.numpy as jnp
from jax import lax
from jax.experimental import pallas as pl
from jax.experimental.pallas import tpu as pltpu
from jax.sharding import PartitionSpec as P

KC = 7
PX = 8
PY = 16
RUNS = 8
AXY = 32
PLANE = PX * PY
BS = 64
HALF = BS // 2
WIDE = 2 * BS
F32 = jnp.float32
BF16 = jnp.bfloat16
NEAR = 5
PITCH = 17


def swap(x):
    return pltpu.roll(x, BS, 1)


def spread(val, low, store):
    turned = swap(val)
    store[pl.ds(0, HALF, stride=2), :] = jnp.where(low, val, turned)
    store[pl.ds(1, HALF, stride=2), :] = jnp.where(low, turned, val)
    return turned


def align_kernel(scal, a_ref, p_ref, near, far, prel, plhs, tmp, vtmp):
    step = pl.program_id(0)
    rows = a_ref.shape[1]
    low = lax.broadcasted_iota(jnp.int32, (HALF, WIDE), 1) < BS
    for k in range(KC):
        for i in range(HALF):
            tmp[k, i * PITCH : i * PITCH + rows, :] = a_ref[k, :, i * WIDE : (i + 1) * WIDE].astype(F32)
    for i in range(HALF):
        tmp[KC, i * PITCH : i * PITCH + rows, :] = p_ref[:, i * WIDE : (i + 1) * WIDE].astype(F32)
    for r in range(rows):
        for j in range(KC):
            k = scal[(step * rows + r) * KC + j]
            block = tmp[k, pl.ds(r, HALF, stride=PITCH), :].astype(BF16)
            if j < NEAR:
                near[j, r] = block
            else:
                far[j - NEAR, r] = block
        val = tmp[KC, pl.ds(r, HALF, stride=PITCH), :]
        turned = spread(val, low, vtmp.at[r])
        prel[r] = vtmp[r].astype(BF16)
        plhs[r // 2, r % 2, 0] = val.astype(BF16)
        plhs[r // 2, r % 2, 1] = turned.astype(BF16)


def aligned(a_blocks, p_blocks, chosen):
    rows = 16
    count, flat = p_blocks.shape
    return pl.pallas_call(
        align_kernel,
        out_shape=(
            jax.ShapeDtypeStruct((NEAR, count, HALF, WIDE), BF16),
            jax.ShapeDtypeStruct((KC - NEAR, count, HALF, WIDE), BF16),
            jax.ShapeDtypeStruct((count, BS, WIDE), BF16),
            jax.ShapeDtypeStruct((count // 2, 2, 2, HALF, WIDE), BF16),
        ),
        grid_spec=pltpu.PrefetchScalarGridSpec(
            num_scalar_prefetch=1,
            grid=(count // rows,),
            in_specs=[
                pl.BlockSpec((KC, rows, flat), lambda s, _: (0, s, 0)),
                pl.BlockSpec((rows, flat), lambda s, _: (s, 0)),
            ],
            out_specs=(
                pl.BlockSpec((NEAR, rows, HALF, WIDE), lambda s, _: (0, s, 0, 0)),
                pl.BlockSpec((KC - NEAR, rows, HALF, WIDE), lambda s, _: (0, s, 0, 0)),
                pl.BlockSpec((rows, BS, WIDE), lambda s, _: (s, 0, 0)),
                pl.BlockSpec((rows // 2, 2, 2, HALF, WIDE), lambda s, _: (s, 0, 0, 0, 0)),
            ),
            scratch_shapes=[
                pltpu.VMEM((KC + 1, PITCH * HALF, WIDE), F32),
                pltpu.VMEM((rows, BS, WIDE), F32),
            ],
        ),
        compiler_params=pltpu.CompilerParams(vmem_limit_bytes=16 * 1024 * 1024),
        cost_estimate=pl.CostEstimate(
            flops=0, bytes_accessed=5 * KC * count * flat, transcendentals=0
        ),
        name="align_blocks",
    )(chosen, a_blocks, p_blocks)


def lane_masks():
    low = lax.broadcasted_iota(jnp.int32, (HALF, WIDE), 1) < BS
    low2 = lax.broadcasted_iota(jnp.int32, (BS, WIDE), 1) < BS
    return low, low2


def both(block, low2):
    dup = block.astype(F32)
    top = jnp.where(low2, dup, 0.0)
    bottom = jnp.where(low2, 0.0, dup)
    return jnp.concatenate([top, bottom], axis=0).astype(BF16)


def pair(a, b, low):
    return jnp.concatenate(
        [jnp.where(low, a, swap(b)), jnp.where(low, swap(a), b)], axis=0
    ).astype(BF16)


def add_product(acc, plhs, at, q, parts):
    lhs = plhs[at].reshape(2 * BS, WIDE)[:, :BS]
    for b, part in enumerate(parts):
        acc[q, b] += lax.dot_general(
            lhs,
            jnp.concatenate(part, axis=0),
            (((0,), (0,)), ((), ())),
            preferred_element_type=F32,
        )


def write_rows(scal, acc, out_ref, low):
    def write_row(o, _):
        q = scal[3 * PY + o]
        for b in range(2):
            even = acc[q, b, pl.ds(0, HALF, stride=2), :]
            odd = acc[q, b, pl.ds(1, HALF, stride=2), :]
            out_ref[o, 2 * b] = jnp.where(low, even, swap(odd)).astype(out_ref.dtype)
            if b == 0:
                out_ref[o, 1] = jnp.where(low, swap(even), odd).astype(out_ref.dtype)
        return 0

    lax.fori_loop(0, AXY, write_row, 0)


def outer_x(x):
    return (x - 1) % PX if x % 2 == 0 else (x + 1) % PX


def far_kernel(scal, blocks, p_own, p_out, plhs, out_ref, carried, acc):
    low, low2 = lane_masks()

    def carry_row(y, _):
        for x in range(PX):
            g = y * PX + x
            f = y * PX + outer_x(x)
            carried[0, f] = jnp.dot(blocks[0, f], both(p_own[g], low2), preferred_element_type=F32)
            carried[1, g] = jnp.dot(blocks[1, g], both(p_out[g], low2), preferred_element_type=F32)
        return 0

    lax.fori_loop(0, PY, carry_row, 0)
    acc[...] = jnp.zeros_like(acc)

    def sum_row(y, _):
        run = scal[y]
        zero = jnp.zeros((HALF, WIDE), F32)
        for c in range(PX // 2):
            parts = ([], [])
            for e in range(2):
                f = y * PX + 2 * c + e
                side = carried[0, f]
                parts[0].append(pair(side, zero, low) if e == 0 else pair(zero, side, low))
                parts[1].append(pair(carried[1, f], zero, low))
            add_product(acc, plhs, (y * PX) // 2 + c, c * RUNS + run, parts)
        return 0

    lax.fori_loop(0, PY, sum_row, 0)
    write_rows(scal, acc, out_ref, low)


def near_kernel(scal, blocks, p_own, zin_ref, plhs, out_ref, ptmp, vtmp, pin, carried, acc):
    low, low2 = lane_masks()
    rows = 16

    def some(n, _):
        part = zin_ref[pl.ds(pl.multiple_of(n * rows, rows), rows), :]
        for i in range(HALF):
            ptmp[i * PITCH : i * PITCH + rows, :] = part[:, i * WIDE : (i + 1) * WIDE].astype(F32)
        for r in range(rows):
            spread(ptmp[pl.ds(r, HALF, stride=PITCH), :], low, vtmp.at[r])
            pin[n * rows + r] = vtmp[r].astype(BF16)
        return 0

    lax.fori_loop(0, PLANE // rows, some, 0)

    def carry_row(y, _):
        above = lax.rem(y + 1, PY)
        below = lax.rem(y + PY - 1, PY)
        for x in range(PX):
            g = y * PX + x
            takers = (g, y * PX + (x ^ 1), above * PX + x, below * PX + x)
            lhs = jnp.concatenate([blocks[j, f] for j, f in enumerate(takers)], axis=0)
            got = jnp.dot(lhs, both(p_own[g], low2), preferred_element_type=F32).astype(BF16)
            for j, f in enumerate(takers):
                carried[j, f] = got[j * HALF : (j + 1) * HALF]
            carried[4, g] = jnp.dot(
                blocks[4, g], both(pin[g], low2), preferred_element_type=F32
            ).astype(BF16)
        return 0

    lax.fori_loop(0, PY, carry_row, 0)
    acc[...] = jnp.zeros_like(acc)

    def sum_row(y, _):
        run = scal[y]
        down_in = scal[PY + y] != 0
        up_in = scal[2 * PY + y] != 0
        zero = jnp.zeros((HALF, WIDE), F32)
        for c in range(PX // 2):
            parts = ([], [])
            for e in range(2):
                f = y * PX + 2 * c + e
                own, inner, down, up, zin = (carried[j, f].astype(F32) for j in range(NEAR))
                kept = (own + inner) + zin
                kept = kept + jnp.where(down_in, down, zero) + jnp.where(up_in, up, zero)
                down = jnp.where(down_in, zero, down)
                up = jnp.where(up_in, zero, up)
                parts[0].append(pair(down, up, low))
                parts[1].append(pair(kept, zero, low))
            add_product(acc, plhs, (y * PX) // 2 + c, c * RUNS + run, parts)
        return 0

    lax.fori_loop(0, PY, sum_row, 0)
    write_rows(scal, acc, out_ref, low)


def layer_part(kernel, name, layer, dtype, scalars, blocks, prel, plhs, zin=None):
    count = blocks.shape[0]
    flat = BS * BS
    plane = pl.BlockSpec((PLANE, BS, WIDE), lambda s, _: (layer, 0, 0))
    if zin is None:
        last = (pl.BlockSpec((PLANE, BS, WIDE), lambda s, _: (1 - layer, 0, 0)), prel)
        scratch = [pltpu.VMEM((KC - NEAR, PLANE, HALF, WIDE), F32)]
    else:
        last = (pl.BlockSpec((PLANE, flat), lambda s, _: (0, 0)), zin)
        scratch = [
            pltpu.VMEM((PITCH * HALF, WIDE), F32),
            pltpu.VMEM((16, BS, WIDE), F32),
            pltpu.VMEM((PLANE, BS, WIDE), BF16),
            pltpu.VMEM((NEAR, PLANE, HALF, WIDE), BF16),
        ]
    return pl.pallas_call(
        kernel,
        out_shape=jax.ShapeDtypeStruct((AXY, 3, HALF, WIDE), dtype),
        grid_spec=pltpu.PrefetchScalarGridSpec(
            num_scalar_prefetch=1,
            grid=(1,),
            in_specs=[
                pl.BlockSpec((count, PLANE, HALF, WIDE), lambda s, _: (0, layer, 0, 0)),
                plane,
                last[0],
                pl.BlockSpec((PLANE // 2, 2, 2, HALF, WIDE), lambda s, _: (layer, 0, 0, 0, 0)),
            ],
            out_specs=pl.BlockSpec((AXY, 3, HALF, WIDE), lambda s, _: (0, 0, 0, 0)),
            scratch_shapes=scratch + [pltpu.VMEM((AXY, 2, BS, WIDE), F32)],
        ),
        compiler_params=pltpu.CompilerParams(vmem_limit_bytes=(28 if zin is None else 37) * 1024 * 1024),
        cost_estimate=pl.CostEstimate(
            flops=PLANE * count * 64 * BS**3,
            bytes_accessed=PLANE * count * flat * 2,
            transcendentals=0,
        ),
        name=name + ("_upper" if layer else "_lower"),
    )(scalars, blocks, prel, last[1], plhs)


def flat_kernel(in_ref, *refs):
    out_ref, tmp = refs[-2:]
    rows = in_ref.shape[0]
    for o in range(rows):
        tmp[o * (HALF + 1) : o * (HALF + 1) + HALF] = in_ref[o, 0].astype(F32)
    for i in range(HALF):
        out_ref[0, :, i * WIDE : (i + 1) * WIDE] = tmp[pl.ds(i, rows, stride=HALF + 1), :].astype(BF16)


def flattened(blocks, slot_of_part, into=None):
    rows, parts = blocks.shape[:2]
    flat = BS * BS
    kept = [] if into is None else [into]
    return pl.pallas_call(
        flat_kernel,
        out_shape=jax.ShapeDtypeStruct((KC, rows, flat), BF16),
        grid=(parts,),
        in_specs=[pl.BlockSpec((rows, 1, HALF, WIDE), lambda s: (0, s, 0, 0))]
        + [pl.BlockSpec(memory_space=pl.ANY) for _ in kept],
        out_specs=pl.BlockSpec((1, rows, flat), lambda s: (slot_of_part(s), 0, 0)),
        scratch_shapes=[pltpu.VMEM((rows * (HALF + 1), WIDE), F32)],
        input_output_aliases={1: 0} if kept else {},
        name="flatten_" + ("near" if kept else "far"),
    )(blocks, *kept)


def per_device(a_blocks, a_cols, p_blocks, p_cols, coarse_owner):
    axes = ("slab", "grp")
    layers = lax.axis_size(axes)
    position = lax.axis_index(axes)
    depth_total = 2 * layers
    up = [(i, (i + 1) % layers) for i in range(layers)]
    down = [(j, i) for i, j in up]
    plane0 = p_blocks[:PLANE]
    plane1 = p_blocks[PLANE:]
    after = lax.ppermute(plane0, axes, down)
    before = lax.ppermute(plane1, axes, up)

    depth = 2 * position + lax.broadcasted_iota(jnp.int32, (2, PY, PX), 0)
    ypos = lax.broadcasted_iota(jnp.int32, (2, PY, PX), 1)
    xpos = lax.broadcasted_iota(jnp.int32, (2, PY, PX), 2)

    def locate(zz, yy, xx):
        return ((zz % depth_total * PY + yy % PY) * PX + xx % PX).reshape(2, PLANE)

    beside = [
        locate(depth, ypos, xpos),
        locate(depth, ypos, xpos + 1 - 2 * (xpos % 2)),
        locate(depth, ypos - 1, xpos),
        locate(depth, ypos + 1, xpos),
    ]
    below, over = locate(depth - 1, ypos, xpos), locate(depth + 1, ypos, xpos)
    beside.append(jnp.stack([below[0], over[1]]))
    beside.append(locate(depth, ypos, xpos - 1 + 2 * (xpos % 2)))
    beside.append(jnp.stack([over[0], below[1]]))
    expected = jnp.stack(beside, axis=2)
    matches = a_cols.reshape(2, PLANE, 1, KC) == expected[..., None]
    chosen = jnp.sum(jnp.where(matches, jnp.arange(KC, dtype=jnp.int32), 0), axis=3)

    runs = p_cols[:PLANE].reshape(PY, PX)[:, 0] % RUNS
    down_in = (jnp.roll(runs, 1) == runs).astype(jnp.int32)
    up_in = (jnp.roll(runs, -1) == runs).astype(jnp.int32)

    def scalars(layer):
        owners = lax.dynamic_index_in_dim(
            coarse_owner, (position + layer) % layers, 0, keepdims=False
        )
        order = jnp.arange(AXY, dtype=jnp.int32)
        picked = jnp.sum(jnp.where(owners[None, :] == order[:, None], order[None, :], 0), axis=1)
        return jnp.concatenate([runs, down_in, up_in, picked])

    near, far, prel, plhs = aligned(jnp.transpose(a_blocks, (1, 0, 2)), p_blocks, chosen.reshape(-1))
    scal = (scalars(0), scalars(1))
    after, before, far = lax.optimization_barrier((after, before, far))

    def exchanged(rows):
        return lax.all_to_all(rows, "slab", split_axis=0, concat_axis=0, tiled=True)

    upper = layer_part(far_kernel, "far", 1, BF16, scal[1], far, prel, plhs)
    arrived = lax.ppermute(upper, axes, up)
    lower = layer_part(far_kernel, "far", 0, F32, scal[0], far, prel, plhs)
    sides = (lower[:, :2] + arrived[:, :2].astype(F32)).astype(BF16)
    far_rows = jnp.concatenate([sides, arrived[:, 2:], lower[:, 2:].astype(BF16)], axis=1)
    far_rows, near = lax.optimization_barrier((far_rows, near))
    far_rows = exchanged(far_rows)

    upper = layer_part(near_kernel, "near", 1, BF16, scal[1], near, prel, plhs, after)
    arrived = lax.ppermute(upper, axes, up)
    lower = layer_part(near_kernel, "near", 0, F32, scal[0], near, prel, plhs, before)
    near_rows = exchanged((lower + arrived.astype(F32)).astype(BF16))

    flat = flattened(far_rows, lambda s: jnp.where(s < 2, s + 1, s + 3))
    flat = flattened(near_rows, lambda s: jnp.where(s < 2, s + 3, 0), flat)
    return jnp.transpose(flat, (1, 0, 2))


def solution(mesh):
    return jax.shard_map(
        per_device,
        mesh=mesh,
        in_specs=(
            P(("slab", "grp"), None, None),
            P(("slab", "grp"), None),
            P(("slab", "grp"), None),
            P(("slab", "grp")),
            P(),
        ),
        out_specs=P(("slab", "grp"), None, None),
        check_vma=False,
    )
```
